32 devices in a mesh: row: 16 (over z, x, core), col: 2 (over y).
Axes of the slice: x: 2, y: 2, z: 4, core: 2. Of those that a mesh axis runs over, the one named last changes fastest.
Arguments:
- features: bfloat16 [8192, 602], P(('row', 'col')), may hold values from -6 to 6
- weight: bfloat16 [602, 256], replicated, may hold values from -0.25 to 0.25
- adj_tiles: bfloat16 [16, 2, 16, 6, 128, 128], P('row', 'col'), may hold values from 0.00077819824 to 0.03125
- tile_row: int32 [16, 2, 16, 6], P('row', 'col'), may hold values from 0 to 3, as said below
- tile_col: int32 [16, 2, 16, 6], P('row', 'col'), may hold values from 0 to 1
- tile_count: int32 [16, 2, 16], P('row', 'col'), may hold values from 1 to 6, as said below
- train_mask: int32 [8192], P(('row', 'col')), may hold values 0 or 1
- cotangent: bfloat16 [8192, 256], P(('row', 'col')), may hold values from -6 to 6
Outputs:
- hidden: bfloat16 [8192, 256], P(('row', 'col'))
- grad_features: bfloat16 [8192, 602], P(('row', 'col'))
- grad_weight: float32 [602, 256], replicated
The draws below stay inside these ranges and needn't reach their ends.
Inputs may be any that keep to these rules, and one draw needn't show every extreme that they name: For each [r, c, j], the pairs (tile_row, tile_col) of the slots are distinct. tile_count[r, c, r] = 6 for every r and c.
All inputs are finite; a program needn't handle non-finite values. No bound on the sum of `train_mask` on one device may be relied on, other than what follows from the above.
Results may differ from the reference program's by a relative error of at most 0.0075.
Values may be sent and summed in bfloat16 or wider, within the bound.
A program may use at most 128 MiB of HBM per device.

```python
import math
import jax
import jax.numpy as jnp
from jax import lax

F_IN = 602
HID = 256
TILE = 128
BLOCK_TILES = 2
SLOTS = 6
ROW_TILES = 4
NODES = 8192
N_ROW = 16
N_COL = 2


def tile_positions(key):
    key_list = jax.random.split(key, N_ROW * N_COL * N_ROW)
    shuffled = jax.vmap(lambda one_key: jax.random.permutation(one_key, ROW_TILES * BLOCK_TILES))(key_list)
    return shuffled[:, :SLOTS].reshape(N_ROW, N_COL, N_ROW, SLOTS).astype(jnp.int32)


def draw_tile_row(key, part):
    placed = tile_positions(key)
    return (placed // BLOCK_TILES).astype(jnp.int32)


def draw_tile_col(key, part):
    placed = tile_positions(key)
    return (placed % BLOCK_TILES).astype(jnp.int32)


def draw_tile_count(key, part):
    key = jax.random.fold_in(key, 3)
    first_key, second_key = jax.random.split(key)
    device_limit = jax.random.randint(first_key, (N_ROW, N_COL, 1), (SLOTS + 1) // 2, SLOTS + 1)
    raw_count = jax.random.randint(second_key, (N_ROW, N_COL, N_ROW), 1, SLOTS + 1)
    clipped = jnp.minimum(raw_count, device_limit)
    diagonal = jnp.arange(N_ROW)[:, None, None] == jnp.arange(N_ROW)[None, None, :]
    return jnp.where(diagonal, SLOTS, clipped).astype(jnp.int32)


def place_ends(result, own_key, low, largest):
    longest = result.shape.index(max(result.shape))
    spots = []
    for shift in (0, 1):
        where = [jax.random.randint(jax.random.fold_in(own_key, axis), (), 0, length) for axis, length in enumerate(result.shape)]
        where[longest] = (where[longest] + shift) % result.shape[longest]
        spots.append(tuple(where))
    return result.at[spots[0]].set(low).at[spots[1]].set(largest)


def levels(stream_key, extent, cuts, smallest, high):
    def one(dim, parts):
        heights = jax.random.uniform(jax.random.fold_in(jax.random.fold_in(stream_key, 6), dim), (parts,), jnp.float32, smallest / len(cuts), high / len(cuts))
        return jnp.repeat(jnp.exp(heights), extent[dim] // parts).reshape((-1,) + (1,) * (len(extent) - dim - 1))

    gain = one(*cuts[0])
    for cut in cuts[1:]:
        gain = gain * one(*cut)
    return gain


def normal_values(own_key, dims, width, most, cuts=(), held_as=jnp.bfloat16):
    array = jax.random.normal(own_key, dims, jnp.float32) * width
    if len(cuts) > 0:
        array = levels(own_key, dims, cuts, -0.22, 0.18) * array
    return jnp.clip(array, min=-most, max=most).astype(held_as)


def setup_inputs(seed: int = 0) -> dict:
    streams_of = jax.random.split(jax.random.key(seed), 9)
    return {
        "features": normal_values(streams_of[0], (NODES, F_IN), 1.0, 6.0, ((0, 32),)),
        "weight": normal_values(streams_of[1], (F_IN, HID), F_IN ** -0.5, 0.25),
        "adj_tiles": jnp.clip(0.00077819824 + 0.030471802 * jax.random.uniform(streams_of[2], (N_ROW, N_COL, N_ROW, SLOTS, TILE, TILE), jnp.float32) ** levels(streams_of[2], (N_ROW, N_COL, N_ROW, SLOTS, TILE, TILE), ((0, 16), (1, 2)), -0.2, 0.2), 0.00077819824, 0.03125).astype(jnp.bfloat16),
        "tile_row": draw_tile_row(jax.random.fold_in(streams_of[8], 71), 0),
        "tile_col": draw_tile_col(jax.random.fold_in(streams_of[8], 71), 0),
        "tile_count": draw_tile_count(jax.random.fold_in(streams_of[8], 71), 0),
        "train_mask": place_ends((jax.random.randint(streams_of[6], (NODES,), 0, 3) < 2).astype(jnp.int32), jax.random.fold_in(streams_of[6], 1), 0, 1),
        "cotangent": normal_values(streams_of[7], (NODES, HID), 1.0, 6.0, ((0, 32),)),
    }


def reference(features, weight, adj_tiles, tile_row, tile_col, tile_count, train_mask, cotangent):
    precise = lax.Precision.HIGHEST
    projected = jnp.dot(features, weight, preferred_element_type=jnp.float32).astype(jnp.bfloat16)
    blocks = projected.reshape(N_ROW, N_COL, BLOCK_TILES, TILE, HID)
    live_slots = (jnp.arange(SLOTS, dtype=jnp.int32)[None, None, None, :] < tile_count[..., None]).astype(jnp.float32)
    block_pick = jnp.arange(N_ROW, dtype=jnp.int32)[None, :, None]
    column_pick = jnp.arange(N_COL, dtype=jnp.int32)[:, None, None]
    row_range = jnp.arange(ROW_TILES, dtype=jnp.int32)
    col_range = jnp.arange(BLOCK_TILES, dtype=jnp.int32)

    def forward_row(pieces):
        adj_blocks, row_ids, col_ids, live_here = pieces
        picked = blocks[block_pick, column_pick, col_ids].astype(jnp.float32)
        product = jnp.einsum('cjkab,cjkbh->cjkah', adj_blocks.astype(jnp.float32), picked, precision=precise)
        product = product * live_here[..., None, None]
        row_hot = (row_ids[..., None] == row_range).astype(jnp.float32)
        return jnp.einsum('cjkr,cjkah->rah', row_hot, product, precision=precise)
    pre_act = lax.map(forward_row, (adj_tiles, tile_row, tile_col, live_slots)).reshape(NODES, HID)
    gate_value = jax.nn.sigmoid(pre_act)
    hidden = (pre_act * gate_value).astype(jnp.bfloat16)
    grad_pre = (cotangent.astype(jnp.float32) * train_mask.astype(jnp.float32)[:, None] * gate_value * (1.0 + pre_act * (1.0 - gate_value))).astype(jnp.bfloat16)
    grad_blocks = grad_pre.reshape(N_ROW, ROW_TILES, TILE, HID)

    def backward_row(grad_acc, pieces):
        adj_blocks, row_ids, col_ids, live_here, grad_here = pieces
        picked = grad_here[row_ids].astype(jnp.float32)
        product = jnp.einsum('cjkab,cjkah->cjkbh', adj_blocks.astype(jnp.float32), picked, precision=precise)
        product = product * live_here[..., None, None]
        col_hot = (col_ids[..., None] == col_range).astype(jnp.float32)
        partial_value = jnp.einsum('cjkt,cjkbh->jctbh', col_hot, product, precision=precise)
        return (grad_acc + partial_value.reshape(NODES, HID), None)
    grad_acc, _ = lax.scan(backward_row, jnp.zeros((NODES, HID), jnp.float32), (adj_tiles, tile_row, tile_col, live_slots, grad_blocks))
    grad_proj = grad_acc.astype(jnp.bfloat16)
    grad_weight = lax.dot_general(features, grad_proj, (((0,), (0,)), ((), ())), preferred_element_type=jnp.float32) * (1.0 / math.sqrt(NODES))
    grad_features = lax.dot_general(grad_proj, weight, (((1,), (1,)), ((), ())), preferred_element_type=jnp.float32).astype(jnp.bfloat16)
    return (hidden, grad_features, grad_weight)
```

```python
import functools
import math

import jax
import jax.numpy as jnp
from jax import lax
from jax.experimental import pallas as pl
from jax.experimental.pallas import tpu as pltpu
from jax.sharding import PartitionSpec as P

BF16 = jnp.bfloat16
F32 = jnp.float32


def layer_kernel(
    row_count,
    col_count,
    grad_scale,
    trow_ref,
    tcol_ref,
    tcount_ref,
    adj_ref,
    feat_ref,
    weight_ref,
    mask_ref,
    cot_ref,
    hidden_ref,
    gfeat_ref,
    gweight_ref,
    tiles,
    dense,
    held,
    acc,
    col_out,
    col_in,
    grad_t,
    core_out,
    core_in,
    mate_out,
    mate_in,
    line_out,
    line_in,
    feat_pad,
    gw_loc,
    gw_s1,
    gw_r1,
    gw_s2,
    gw_r2,
    gw_line,
    gw_full,
    adj_sem,
    g_line,
    g_mate,
    g_core,
    g_recv,
    c_send,
    c_recv,
    t_send,
    t_recv,
    b_core_send,
    b_core_recv,
    b_mate_send,
    b_mate_recv,
    b_line_send,
    b_line_recv,
    w_send,
    w_recv,
    w_plane_send,
    w_plane_recv,
    w_line_send,
    w_line_recv,
    w_gat_send,
    w_gat_recv,
):
    line_count = row_count // 4
    me = lax.axis_index("row")
    col = lax.axis_index("col")
    core = me % 2
    mate = (me // 2) % 2
    line = me // 4
    slot_count = adj_ref.shape[3]
    tile = adj_ref.shape[4]
    nodes = feat_ref.shape[1]
    block_tiles = nodes // tile

    def row_id(l, m, k):
        return (l * 2 + m) * 2 + k

    def line_at(d):
        return (line + d) % line_count

    to_core = {"row": row_id(line, mate, 1 - core)}
    to_mate = {"row": row_id(line, 1 - mate, core)}

    def to_line(d):
        return {"row": row_id(line_at(d), mate, core)}

    def to_col(d):
        return {"col": (col + d) % col_count}

    plane = [(dm, dc) for dm in range(2) for dc in range(col_count) if dm + dc > 0]

    def plane_part(dm, dc):
        return ((mate + dm) % 2) * col_count + (col + dc) % col_count

    def to_plane(dm, dc):
        return {
            "row": row_id(line, (mate + dm) % 2, core),
            "col": (col + dc) % col_count,
        }

    near = sorted(range(1, line_count), key=lambda d: min(d, line_count - d))
    far = near[::-1]
    peers = [to_core, to_mate] + [to_line(d) for d in near]
    peers += [to_col(d) for d in range(1, col_count)]
    peers += [to_plane(1, dc) for dc in range(1, col_count)]

    started = []

    def push(src, dst, send, recv, target):
        copy = pltpu.make_async_remote_copy(
            src_ref=src,
            dst_ref=dst,
            send_sem=send,
            recv_sem=recv,
            device_id=target,
            device_id_type=pl.DeviceIdType.MESH,
        )
        copy.start()
        started.append(copy)

    def arrived(dst, recv):
        pltpu.make_async_remote_copy(
            src_ref=dst,
            dst_ref=dst,
            send_sem=recv,
            recv_sem=recv,
            device_id=to_core,
            device_id_type=pl.DeviceIdType.MESH,
        ).wait_recv()

    adj_copy = pltpu.make_async_copy(
        adj_ref.at[0, 0], tiles.at[:, pl.ds(0, slot_count)], adj_sem
    )
    adj_copy.start()
    barrier = pltpu.get_barrier_semaphore()
    for peer in peers:
        pl.semaphore_signal(
            barrier, inc=1, device_id=peer, device_id_type=pl.DeviceIdType.MESH
        )
    held[me] = lax.dot_general(
        feat_ref[...], weight_ref[...], (((0,), (0,)), ((), ())), preferred_element_type=F32
    ).astype(BF16)
    pl.semaphore_wait(barrier, len(peers))

    own = held.at[me]
    for d in near:
        push(own, own, g_line.at[d], g_recv.at[me], to_line(d))
    push(own, own, g_mate.at[line], g_recv.at[me], to_mate)
    push(own, own, g_core.at[line * 2 + mate], g_recv.at[me], to_core)

    tiles[:, slot_count] = jnp.zeros_like(tiles[:, slot_count])
    adj_copy.wait()

    def build(j, carry):
        filled = []
        for s in range(slot_count):
            live = s < tcount_ref[0, 0, j]
            place = trow_ref[0, 0, s, j] * block_tiles + tcol_ref[0, 0, s, j]
            filled.append(jnp.where(live, place, -1))
        for r in range(col_count * block_tiles):
            for t in range(block_tiles):
                slot = jnp.int32(slot_count)
                for s in range(slot_count):
                    slot = jnp.where(filled[s] == r * block_tiles + t, s, slot)
                dense[
                    j,
                    r // block_tiles,
                    pl.ds((r % block_tiles) * tile, tile),
                    pl.ds(t * tile, tile),
                ] = tiles[j, slot]
        return carry

    lax.fori_loop(0, row_count, build, 0)

    def accumulate(j, first=False):
        def one(i, carry):
            product = jnp.dot(dense[j, i], held[j], preferred_element_type=F32)
            acc[i] = product if first else acc[i] + product
            return carry

        lax.fori_loop(0, col_count, one, 0, unroll=col_count <= 2)

    def forward_mate(l):
        block = row_id(l, mate, core)
        push(held.at[block], held.at[block], g_mate.at[l], g_recv.at[block], to_mate)

    def forward_core(l, m):
        block = row_id(l, m, core)
        push(held.at[block], held.at[block], g_core.at[l * 2 + m], g_recv.at[block], to_core)

    def take(l, m, k):
        block = row_id(l, m, k)
        arrived(held.at[block], g_recv.at[block])
        return block

    accumulate(me, first=True)
    accumulate(take(line, mate, 1 - core))
    late = []
    last_line = line
    for d in near:
        l = line_at(d)
        block = take(l, mate, core)
        forward_mate(l)
        forward_core(l, mate)
        crossed = take(last_line, 1 - mate, core)
        forward_core(last_line, 1 - mate)
        for item in late:
            accumulate(take(*item))
        accumulate(block)
        accumulate(crossed)
        late = [(l, mate, 1 - core), (last_line, 1 - mate, 1 - core)]
        last_line = l
    for item in late:
        accumulate(take(*item))
    crossed = take(last_line, 1 - mate, core)
    forward_core(last_line, 1 - mate)
    accumulate(crossed)
    accumulate(take(last_line, 1 - mate, 1 - core))

    for d in range(1, col_count):
        col_out[d] = acc[(col + d) % col_count].astype(BF16)
        push(col_out.at[d], col_in.at[d], c_send.at[d], c_recv.at[d], to_col(d))
    width = feat_ref.shape[0]
    pad_from = (width // 16) * 16
    feat_pad[pad_from:, :] = jnp.zeros_like(feat_pad[pad_from:, :])
    feat_pad[:width, :] = feat_ref[...]
    pre_act = acc[col]
    for d in range(1, col_count):
        arrived(col_in.at[d], c_recv.at[d])
        pre_act = pre_act + col_in[d].astype(F32)

    gate = jax.nn.sigmoid(pre_act)
    grad_pre = cot_ref[...].astype(F32) * gate * (1.0 + pre_act * (1.0 - gate))
    grad_t[col] = (grad_pre.T * mask_ref[...].astype(F32)).astype(BF16)
    for d in range(1, col_count):
        push(grad_t.at[col], grad_t.at[col], t_send.at[d], t_recv.at[col], to_col(d))
    hidden_ref[...] = (pre_act * gate).astype(BF16)
    for d in range(1, col_count):
        other = (col + d) % col_count
        arrived(grad_t.at[other], t_recv.at[other])

    def partial_sum(block):
        def one(i, running):
            return running + jnp.dot(grad_t[i], dense[block, i], preferred_element_type=F32)

        start = jnp.dot(grad_t[0], dense[block, 0], preferred_element_type=F32)
        return lax.fori_loop(1, col_count, one, start, unroll=col_count <= 2)

    order = far + [0]

    def send_core(side):
        for d in order:
            l = line_at(d)
            at = l * 2 + side
            core_out[at] = partial_sum(row_id(l, side, 1 - core)).astype(BF16)
            push(core_out.at[at], core_in.at[at], b_core_send.at[at], b_core_recv.at[at], to_core)

    send_core(1 - mate)
    for d in order:
        l = line_at(d)
        at = l * 2 + 1 - mate
        mine = partial_sum(row_id(l, 1 - mate, core))
        arrived(core_in.at[at], b_core_recv.at[at])
        mate_out[l] = (mine + core_in[at].astype(F32)).astype(BF16)
        push(mate_out.at[l], mate_in.at[l], b_mate_send.at[l], b_mate_recv.at[l], to_mate)
    send_core(mate)
    total = None
    for d in order:
        l = line_at(d)
        at = l * 2 + mate
        mine = partial_sum(row_id(l, mate, core))
        arrived(core_in.at[at], b_core_recv.at[at])
        mine = mine + core_in[at].astype(F32)
        arrived(mate_in.at[l], b_mate_recv.at[l])
        mine = mine + mate_in[l].astype(F32)
        if d:
            line_out[d] = mine.astype(BF16)
            push(line_out.at[d], line_in.at[d], b_line_send.at[d], b_line_recv.at[d], to_line(d))
        else:
            total = mine
    for d in far:
        arrived(line_in.at[d], b_line_recv.at[d])
        total = total + line_in[d].astype(F32)

    wire = gw_full.dtype
    proj_t = total.astype(BF16)
    local = lax.dot_general(
        proj_t, feat_pad[...], (((1,), (1,)), ((), ())), preferred_element_type=F32
    )
    gw_loc[...] = (local * grad_scale).reshape(gw_loc.shape)
    gw_s1[...] = gw_loc[1 - core].astype(wire)
    push(gw_s1, gw_r1, w_send.at[0], w_recv.at[0], to_core)
    gfeat_ref[...] = jnp.dot(weight_ref[...], proj_t, preferred_element_type=F32).astype(BF16)
    arrived(gw_r1, w_recv.at[0])
    for dm, dc in plane[::-1]:
        at = dm * col_count + dc
        p = plane_part(dm, dc)
        gw_s2[at] = (gw_loc[core, p] + gw_r1[p].astype(F32)).astype(wire)
        push(gw_s2.at[at], gw_r2.at[at], w_plane_send.at[at], w_plane_recv.at[at], to_plane(dm, dc))
    own_part = plane_part(0, 0)
    part = gw_loc[core, own_part] + gw_r1[own_part].astype(F32)
    for dm, dc in plane:
        at = dm * col_count + dc
        arrived(gw_r2.at[at], w_plane_recv.at[at])
        part = part + gw_r2[at].astype(F32)
    gw_line[line] = part.astype(wire)
    for d in far:
        push(gw_line.at[line], gw_line.at[line], w_line_send.at[d], w_line_recv.at[line], to_line(d))
    for d in near:
        l = line_at(d)
        arrived(gw_line.at[l], w_line_recv.at[l])
    part = gw_line[0].astype(F32)
    for i in range(1, line_count):
        part = part + gw_line[i].astype(F32)
    gw_full[core, own_part] = part.astype(wire)
    mine = gw_full.at[core, own_part]
    for dm, dc in plane[::-1]:
        at = dm * col_count + dc
        push(mine, mine, w_gat_send.at[at], w_gat_recv.at[own_part], to_plane(dm, dc))
    for dm, dc in plane:
        p = plane_part(dm, dc)
        arrived(gw_full.at[core, p], w_gat_recv.at[p])
    mine = gw_full.at[core]
    push(mine, mine, w_send.at[1], w_recv.at[1], to_core)
    arrived(gw_full.at[1 - core], w_recv.at[1])
    gweight_ref[...] = gw_full[...].reshape(gweight_ref.shape[1], gweight_ref.shape[0]).T

    for copy in started:
        copy.wait_send()


def body(features, weight, adj_tiles, tile_row, tile_col, tile_count, train_mask, cotangent):
    rows = lax.axis_size("row")
    cols = lax.axis_size("col")
    slot_count, tile = adj_tiles.shape[3], adj_tiles.shape[4]
    nodes, width = features.shape
    hid = weight.shape[1]
    lines = rows // 4
    padded = -(-width // 128) * 128
    parts = 2 * cols
    piece = hid // (2 * parts)
    wire = BF16 if piece % 16 == 0 else F32
    grad_scale = 1.0 / math.sqrt(rows * cols * nodes)

    vmem = pltpu.VMEM
    sems = lambda n: pltpu.SemaphoreType.DMA((n,))
    scratch = [
        vmem((rows, slot_count + 1, tile, tile), BF16),
        vmem((rows, cols, nodes, nodes), BF16),
        vmem((rows, nodes, hid), BF16),
        vmem((cols, nodes, hid), F32),
        vmem((cols, nodes, hid), BF16),
        vmem((cols, nodes, hid), BF16),
        vmem((cols, hid, nodes), BF16),
        vmem((rows // 2, hid, nodes), BF16),
        vmem((rows // 2, hid, nodes), BF16),
        vmem((lines, hid, nodes), BF16),
        vmem((lines, hid, nodes), BF16),
        vmem((lines, hid, nodes), BF16),
        vmem((lines, hid, nodes), BF16),
        vmem((padded, nodes), BF16),
        vmem((2, parts, piece, padded), F32),
        vmem((parts, piece, padded), wire),
        vmem((parts, piece, padded), wire),
        vmem((parts, piece, padded), wire),
        vmem((parts, piece, padded), wire),
        vmem((lines, piece, padded), wire),
        vmem((2, parts, piece, padded), wire),
        pltpu.SemaphoreType.DMA,
        sems(lines),
        sems(lines),
        sems(rows // 2),
        sems(rows),
        sems(cols),
        sems(cols),
        sems(cols),
        sems(cols),
        sems(rows // 2),
        sems(rows // 2),
        sems(lines),
        sems(lines),
        sems(lines),
        sems(lines),
        sems(2),
        sems(2),
        sems(parts),
        sems(parts),
        sems(lines),
        sems(lines),
        sems(parts),
        sems(parts),
    ]
    whole = pl.BlockSpec(memory_space=pltpu.VMEM)
    hidden, grad_features, grad_weight = pl.pallas_call(
        functools.partial(layer_kernel, rows, cols, grad_scale),
        out_shape=(
            jax.ShapeDtypeStruct((nodes, hid), BF16),
            jax.ShapeDtypeStruct((width, nodes), BF16),
            jax.ShapeDtypeStruct((padded, hid), wire),
        ),
        in_specs=[
            pl.BlockSpec(memory_space=pltpu.SMEM),
            pl.BlockSpec(memory_space=pltpu.SMEM),
            pl.BlockSpec(memory_space=pltpu.SMEM),
            pl.BlockSpec(memory_space=pl.ANY),
            whole,
            whole,
            whole,
            whole,
        ],
        out_specs=(whole, whole, whole),
        scratch_shapes=scratch,
        compiler_params=pltpu.CompilerParams(
            collective_id=0, has_side_effects=True, vmem_limit_bytes=63 * 1024 * 1024
        ),
        name="graph_layer",
    )(
        tile_row.swapaxes(2, 3),
        tile_col.swapaxes(2, 3),
        tile_count,
        adj_tiles,
        features.T,
        weight,
        train_mask.reshape(1, nodes),
        cotangent,
    )
    return (hidden, grad_features.T, grad_weight[:width].astype(F32))


def solution(mesh):
    in_specs = (
        P(("row", "col"), None),
        P(),
        P("row", "col", None, None, None, None),
        P("row", "col", None, None),
        P("row", "col", None, None),
        P("row", "col", None),
        P(("row", "col")),
        P(("row", "col"), None),
    )
    out_specs = (P(("row", "col"), None), P(("row", "col"), None), P())
    return jax.shard_map(body, mesh=mesh, in_specs=in_specs, out_specs=out_specs, check_vma=False)
```

```python
import functools
import math

import jax
import jax.numpy as jnp
from jax import lax
from jax.experimental import pallas as pl
from jax.experimental.pallas import tpu as pltpu
from jax.sharding import PartitionSpec as P

BF16 = jnp.bfloat16
F32 = jnp.float32


def layer_kernel(
    row_count,
    col_count,
    grad_scale,
    halves,
    trow_ref,
    tcol_ref,
    tcount_ref,
    adj_ref,
    feat_ref,
    weight_ref,
    mask_ref,
    cot_ref,
    hidden_ref,
    gfeat_ref,
    gweight_ref,
    tiles,
    dense,
    held,
    acc,
    col_out,
    col_in,
    grad_t,
    grad_cat,
    core_out,
    core_in,
    mate_out,
    mate_in,
    line_out,
    line_in,
    own_sum,
    proj_t,
    feat_pad,
    gw_loc,
    gw_s1,
    gw_r1,
    gw_s2,
    gw_r2,
    gw_line,
    gw_full,
    adj_sem,
    g_line,
    g_mate,
    g_core,
    g_recv,
    c_send,
    c_recv,
    t_send,
    t_recv,
    b_core_send,
    b_core_recv,
    b_mate_send,
    b_mate_recv,
    b_line_send,
    b_line_recv,
    w_send,
    w_recv,
    w_plane_send,
    w_plane_recv,
    w_line_send,
    w_line_recv,
    w_gat_send,
    w_gat_recv,
):
    line_count = row_count // 4
    me = lax.axis_index("row")
    col = lax.axis_index("col")
    core = me % 2
    mate = (me // 2) % 2
    line = me // 4
    slot_count = adj_ref.shape[3]
    tile = adj_ref.shape[4]
    nodes = feat_ref.shape[1]
    block_tiles = nodes // tile
    hid = weight_ref.shape[1] // halves

    def row_id(l, m, k):
        return (l * 2 + m) * 2 + k

    def line_at(d):
        return (line + d) % line_count

    to_core = {"row": row_id(line, mate, 1 - core)}
    to_mate = {"row": row_id(line, 1 - mate, core)}

    def to_line(d):
        return {"row": row_id(line_at(d), mate, core)}

    def to_col(d):
        return {"col": (col + d) % col_count}

    plane = [(dm, dc) for dm in range(2) for dc in range(col_count) if dm + dc > 0]

    def plane_part(dm, dc):
        return ((mate + dm) % 2) * col_count + (col + dc) % col_count

    def to_plane(dm, dc):
        return {
            "row": row_id(line, (mate + dm) % 2, core),
            "col": (col + dc) % col_count,
        }

    near = sorted(range(1, line_count), key=lambda d: min(d, line_count - d))
    far = near[::-1]
    peers = [to_core, to_mate] + [to_line(d) for d in near]
    peers += [to_col(d) for d in range(1, col_count)]
    peers += [to_plane(1, dc) for dc in range(1, col_count)]

    started = []

    def push(src, dst, send, recv, target):
        copy = pltpu.make_async_remote_copy(
            src_ref=src,
            dst_ref=dst,
            send_sem=send,
            recv_sem=recv,
            device_id=target,
            device_id_type=pl.DeviceIdType.MESH,
        )
        copy.start()
        started.append(copy)

    def arrived(dst, recv):
        pltpu.make_async_remote_copy(
            src_ref=dst,
            dst_ref=dst,
            send_sem=recv,
            recv_sem=recv,
            device_id=to_core,
            device_id_type=pl.DeviceIdType.MESH,
        ).wait_recv()

    adj_copy = pltpu.make_async_copy(
        adj_ref.at[0, 0], tiles.at[:, pl.ds(0, slot_count)], adj_sem
    )
    adj_copy.start()
    barrier = pltpu.get_barrier_semaphore()
    for peer in peers:
        pl.semaphore_signal(
            barrier, inc=1, device_id=peer, device_id_type=pl.DeviceIdType.MESH
        )
    projected = lax.dot_general(
        feat_ref[...], weight_ref[...], (((0,), (0,)), ((), ())), preferred_element_type=F32
    ).astype(BF16)
    for h in range(halves):
        held[h, me] = projected[:, h * hid : (h + 1) * hid]
    pl.semaphore_wait(barrier, len(peers))

    def send_own(h):
        own = held.at[h, me]
        for d in near:
            push(own, own, g_line.at[h, d], g_recv.at[h, me], to_line(d))
        push(own, own, g_mate.at[h, line], g_recv.at[h, me], to_mate)
        push(own, own, g_core.at[h, line * 2 + mate], g_recv.at[h, me], to_core)

    send_own(0)
    tiles[:, slot_count] = jnp.zeros_like(tiles[:, slot_count])
    adj_copy.wait()

    def build(j, carry):
        filled = []
        for s in range(slot_count):
            live = s < tcount_ref[0, 0, j]
            place = trow_ref[0, s, 0, j] * block_tiles + tcol_ref[0, s, 0, j]
            filled.append(jnp.where(live, place, -1))
        for r in range(col_count * block_tiles):
            for t in range(block_tiles):
                slot = jnp.int32(slot_count)
                for s in range(slot_count):
                    slot = jnp.where(filled[s] == r * block_tiles + t, s, slot)
                dense[j, pl.ds(r * tile, tile), pl.ds(t * tile, tile)] = tiles[j, slot]
        return carry

    if halves == 1:
        lax.fori_loop(0, row_count, build, 0)

    def rows_of(i):
        return pl.ds(pl.multiple_of(i * nodes, nodes), nodes)

    def accumulate(h, j, first=False):
        if halves > 1 and h == 0:
            build(j, 0)
        if col_count <= 2:
            product = jnp.dot(dense[j], held[h, j], preferred_element_type=F32)
            acc[h] = product if first else acc[h] + product
            return

        def one(i, carry):
            product = jnp.dot(dense[j, rows_of(i)], held[h, j], preferred_element_type=F32)
            acc[h, rows_of(i)] = product if first else acc[h, rows_of(i)] + product
            return carry

        lax.fori_loop(0, col_count, one, 0)

    def forward_mate(h, l):
        block = row_id(l, mate, core)
        ref = held.at[h, block]
        push(ref, ref, g_mate.at[h, l], g_recv.at[h, block], to_mate)

    def forward_core(h, l, m):
        block = row_id(l, m, core)
        ref = held.at[h, block]
        push(ref, ref, g_core.at[h, l * 2 + m], g_recv.at[h, block], to_core)

    def take(h, l, m, k):
        block = row_id(l, m, k)
        arrived(held.at[h, block], g_recv.at[h, block])
        return block

    def gather_steps(h):
        accumulate(h, me, first=True)
        if h + 1 < halves:
            send_own(h + 1)
        accumulate(h, take(h, line, mate, 1 - core))
        late = []
        last_line = line
        for d in near:
            l = line_at(d)
            block = take(h, l, mate, core)
            forward_mate(h, l)
            forward_core(h, l, mate)
            crossed = take(h, last_line, 1 - mate, core)
            forward_core(h, last_line, 1 - mate)
            for item in late:
                accumulate(h, take(h, *item))
            accumulate(h, block)
            accumulate(h, crossed)
            late = [(l, mate, 1 - core), (last_line, 1 - mate, 1 - core)]
            last_line = l
            yield
        for item in late:
            accumulate(h, take(h, *item))
        crossed = take(h, last_line, 1 - mate, core)
        forward_core(h, last_line, 1 - mate)
        accumulate(h, crossed)
        accumulate(h, take(h, last_line, 1 - mate, 1 - core))

    def col_send(h):
        for d in range(1, col_count):
            col_out[h, d] = acc[h, rows_of((col + d) % col_count)].astype(BF16)
            push(col_out.at[h, d], col_in.at[h, d], c_send.at[h, d], c_recv.at[h, d], to_col(d))

    def col_finish(h):
        lanes = slice(h * hid, (h + 1) * hid)
        pre_act = acc[h, rows_of(col)]
        for d in range(1, col_count):
            arrived(col_in.at[h, d], c_recv.at[h, d])
            pre_act = pre_act + col_in[h, d].astype(F32)
        gate = jax.nn.sigmoid(pre_act)
        grad_pre = cot_ref[:, lanes].astype(F32) * gate * (1.0 + pre_act * (1.0 - gate))
        grad_t[h, col] = (grad_pre.T * mask_ref[...].astype(F32)).astype(BF16)
        mine = grad_t.at[h, col]
        for d in range(1, col_count):
            push(mine, mine, t_send.at[h, d], t_recv.at[h, col], to_col(d))
        hidden_ref[:, lanes] = (pre_act * gate).astype(BF16)

    def col_take(h):
        for d in range(1, col_count):
            other = (col + d) % col_count
            arrived(grad_t.at[h, other], t_recv.at[h, other])
        for i in range(col_count):
            grad_cat[h, :, i * nodes : (i + 1) * nodes] = grad_t[h, i]

    def partial_sum(h, block):
        if col_count <= 2:
            return jnp.dot(grad_cat[h], dense[block], preferred_element_type=F32)

        def one(i, running):
            return running + jnp.dot(
                grad_t[h, i], dense[block, rows_of(i)], preferred_element_type=F32
            )

        return lax.fori_loop(0, col_count, one, jnp.zeros((hid, nodes), F32))

    order = far + [0]

    def send_core(h, side):
        for d in order:
            l = line_at(d)
            at = l * 2 + side
            core_out[h, at] = partial_sum(h, row_id(l, side, 1 - core)).astype(BF16)
            push(
                core_out.at[h, at],
                core_in.at[h, at],
                b_core_send.at[h, at],
                b_core_recv.at[h, at],
                to_core,
            )

    def send_mate(h):
        for d in order:
            l = line_at(d)
            at = l * 2 + 1 - mate
            mine = partial_sum(h, row_id(l, 1 - mate, core))
            arrived(core_in.at[h, at], b_core_recv.at[h, at])
            mate_out[h, l] = (mine + core_in[h, at].astype(F32)).astype(BF16)
            push(
                mate_out.at[h, l],
                mate_in.at[h, l],
                b_mate_send.at[h, l],
                b_mate_recv.at[h, l],
                to_mate,
            )

    def send_line(h):
        for d in order:
            l = line_at(d)
            at = l * 2 + mate
            mine = partial_sum(h, row_id(l, mate, core))
            arrived(core_in.at[h, at], b_core_recv.at[h, at])
            mine = mine + core_in[h, at].astype(F32)
            arrived(mate_in.at[h, l], b_mate_recv.at[h, l])
            mine = mine + mate_in[h, l].astype(F32)
            if d:
                line_out[h, d] = mine.astype(BF16)
                push(
                    line_out.at[h, d],
                    line_in.at[h, d],
                    b_line_send.at[h, d],
                    b_line_recv.at[h, d],
                    to_line(d),
                )
            else:
                own_sum[h] = mine

    def finish(h):
        total = own_sum[h]
        for d in far:
            arrived(line_in.at[h, d], b_line_recv.at[h, d])
            total = total + line_in[h, d].astype(F32)
        proj_t[h * hid : (h + 1) * hid, :] = total.astype(BF16)

    def pad_features():
        width = feat_ref.shape[0]
        pad_from = (width // 16) * 16
        feat_pad[pad_from:, :] = jnp.zeros_like(feat_pad[pad_from:, :])
        feat_pad[:width, :] = feat_ref[...]

    wire = gw_full.dtype

    def weight_steps(h):
        local = lax.dot_general(
            proj_t[h * hid : (h + 1) * hid, :],
            feat_pad[...],
            (((1,), (1,)), ((), ())),
            preferred_element_type=F32,
        )
        gw_loc[h] = (local * grad_scale).reshape(gw_loc.shape[1:])
        gw_s1[h] = gw_loc[h, 1 - core].astype(wire)
        push(gw_s1.at[h], gw_r1.at[h], w_send.at[h, 0], w_recv.at[h, 0], to_core)
        yield
        arrived(gw_r1.at[h], w_recv.at[h, 0])
        for dm, dc in plane[::-1]:
            at = dm * col_count + dc
            p = plane_part(dm, dc)
            gw_s2[h, at] = (gw_loc[h, core, p] + gw_r1[h, p].astype(F32)).astype(wire)
            push(
                gw_s2.at[h, at],
                gw_r2.at[h, at],
                w_plane_send.at[h, at],
                w_plane_recv.at[h, at],
                to_plane(dm, dc),
            )
        own_part = plane_part(0, 0)
        part = gw_loc[h, core, own_part] + gw_r1[h, own_part].astype(F32)
        yield
        for dm, dc in plane:
            at = dm * col_count + dc
            arrived(gw_r2.at[h, at], w_plane_recv.at[h, at])
            part = part + gw_r2[h, at].astype(F32)
        gw_line[h, line] = part.astype(wire)
        mine = gw_line.at[h, line]
        for d in far:
            push(mine, mine, w_line_send.at[h, d], w_line_recv.at[h, line], to_line(d))
        yield
        for d in near:
            l = line_at(d)
            arrived(gw_line.at[h, l], w_line_recv.at[h, l])
        part = gw_line[h, 0].astype(F32)
        for i in range(1, line_count):
            part = part + gw_line[h, i].astype(F32)
        gw_full[h, core, own_part] = part.astype(wire)
        mine = gw_full.at[h, core, own_part]
        for dm, dc in plane[::-1]:
            at = dm * col_count + dc
            push(
                mine,
                mine,
                w_gat_send.at[h, at],
                w_gat_recv.at[h, own_part],
                to_plane(dm, dc),
            )
        yield
        for dm, dc in plane:
            p = plane_part(dm, dc)
            arrived(gw_full.at[h, core, p], w_gat_recv.at[h, p])
        mine = gw_full.at[h, core]
        push(mine, mine, w_send.at[h, 1], w_recv.at[h, 1], to_core)
        yield
        arrived(gw_full.at[h, 1 - core], w_recv.at[h, 1])
        full = gw_full[h].reshape(hid, gweight_ref.shape[0])
        gweight_ref[:, h * hid : (h + 1) * hid] = full.T

    def feature_gradient():
        gfeat_ref[...] = jnp.dot(
            weight_ref[...], proj_t[...], preferred_element_type=F32
        ).astype(BF16)

    if halves == 2:
        first, second = gather_steps(0), gather_steps(1)
        for _ in near:
            next(first)
        next(second)
        for _ in first:
            pass
        col_send(0)
        next(second)
        pad_features()
        col_finish(0)
        for _ in second:
            pass
        col_send(1)
        col_take(0)
        send_core(0, 1 - mate)
        col_finish(1)
        send_mate(0)
        send_core(0, mate)
        col_take(1)
        send_core(1, 1 - mate)
        send_line(0)
        send_mate(1)
        send_core(1, mate)
        send_line(1)
        finish(0)
        ahead, behind = weight_steps(0), weight_steps(1)
        next(ahead)
        next(ahead)
        finish(1)
        next(behind)
        for _ in ahead:
            next(behind)
        feature_gradient()
        for _ in behind:
            pass
    else:
        for _ in gather_steps(0):
            pass
        col_send(0)
        pad_features()
        col_finish(0)
        col_take(0)
        send_core(0, 1 - mate)
        send_mate(0)
        send_core(0, mate)
        send_line(0)
        finish(0)
        steps = weight_steps(0)
        next(steps)
        feature_gradient()
        for _ in steps:
            pass

    for copy in started:
        copy.wait_send()


def results_kernel(hidden_in, gfeat_in, gweight_in, hidden_ref, gfeat_ref, gweight_ref):
    hidden_ref[...] = hidden_in[...]
    gfeat_ref[...] = gfeat_in[...]
    gweight_ref[...] = gweight_in[: gweight_ref.shape[0], :].astype(F32)


def body(features, weight, adj_tiles, tile_row, tile_col, tile_count, train_mask, cotangent):
    rows = lax.axis_size("row")
    cols = lax.axis_size("col")
    slot_count, tile = adj_tiles.shape[3], adj_tiles.shape[4]
    nodes, width = features.shape
    hid = weight.shape[1]
    lines = rows // 4
    padded = -(-width // 128) * 128
    parts = 2 * cols
    halves = 2 if hid % (32 * parts) == 0 else 1
    part_hid = hid // halves
    piece = part_hid // (2 * parts)
    wire = BF16 if piece % 16 == 0 else F32
    grad_scale = 1.0 / math.sqrt(rows * cols * nodes)

    vmem = pltpu.VMEM
    half_sems = lambda n: pltpu.SemaphoreType.DMA((halves, n))
    scratch = [
        vmem((rows, slot_count + 1, tile, tile), BF16),
        vmem((rows, cols * nodes, nodes), BF16),
        vmem((halves, rows, nodes, part_hid), BF16),
        vmem((halves, cols * nodes, part_hid), F32),
        vmem((halves, cols, nodes, part_hid), BF16),
        vmem((halves, cols, nodes, part_hid), BF16),
        vmem((halves, cols, part_hid, nodes), BF16),
        vmem((halves, part_hid, cols * nodes), BF16),
        vmem((halves, rows // 2, part_hid, nodes), BF16),
        vmem((halves, rows // 2, part_hid, nodes), BF16),
        vmem((halves, lines, part_hid, nodes), BF16),
        vmem((halves, lines, part_hid, nodes), BF16),
        vmem((halves, lines, part_hid, nodes), BF16),
        vmem((halves, lines, part_hid, nodes), BF16),
        vmem((halves, part_hid, nodes), F32),
        vmem((hid, nodes), BF16),
        vmem((padded, nodes), BF16),
        vmem((halves, 2, parts, piece, padded), F32),
        vmem((halves, parts, piece, padded), wire),
        vmem((halves, parts, piece, padded), wire),
        vmem((halves, parts, piece, padded), wire),
        vmem((halves, parts, piece, padded), wire),
        vmem((halves, lines, piece, padded), wire),
        vmem((halves, 2, parts, piece, padded), wire),
        pltpu.SemaphoreType.DMA,
        half_sems(lines),
        half_sems(lines),
        half_sems(rows // 2),
        half_sems(rows),
        half_sems(cols),
        half_sems(cols),
        half_sems(cols),
        half_sems(cols),
        half_sems(rows // 2),
        half_sems(rows // 2),
        half_sems(lines),
        half_sems(lines),
        half_sems(lines),
        half_sems(lines),
        half_sems(2),
        half_sems(2),
        half_sems(parts),
        half_sems(parts),
        half_sems(lines),
        half_sems(lines),
        half_sems(parts),
        half_sems(parts),
    ]
    whole = pl.BlockSpec(memory_space=pltpu.VMEM)
    hidden, grad_features, grad_weight = pl.pallas_call(
        functools.partial(layer_kernel, rows, cols, grad_scale, halves),
        out_shape=(
            jax.ShapeDtypeStruct((nodes, hid), BF16),
            jax.ShapeDtypeStruct((width, nodes), BF16),
            jax.ShapeDtypeStruct((padded, hid), wire),
        ),
        in_specs=[
            pl.BlockSpec(memory_space=pltpu.SMEM),
            pl.BlockSpec(memory_space=pltpu.SMEM),
            pl.BlockSpec(memory_space=pltpu.SMEM),
            pl.BlockSpec(memory_space=pl.ANY),
            whole,
            whole,
            whole,
            whole,
        ],
        out_specs=(whole, whole, whole),
        scratch_shapes=scratch,
        compiler_params=pltpu.CompilerParams(
            collective_id=0, has_side_effects=True, vmem_limit_bytes=63 * 1024 * 1024
        ),
        name="graph_layer",
    )(
        tile_row.transpose(0, 3, 1, 2),
        tile_col.transpose(0, 3, 1, 2),
        tile_count,
        adj_tiles,
        features.T,
        weight,
        train_mask.reshape(1, nodes),
        cotangent,
    )
    hidden, grad_features, grad_weight = pl.pallas_call(
        results_kernel,
        out_shape=(
            jax.ShapeDtypeStruct((nodes, hid), BF16),
            jax.ShapeDtypeStruct((width, nodes), BF16),
            jax.ShapeDtypeStruct((width, hid), F32),
        ),
        in_specs=[whole] * 3,
        out_specs=(whole, whole, whole),
        name="results",
    )(hidden, grad_features, grad_weight)
    return (hidden, grad_features.T, grad_weight)


def solution(mesh):
    in_specs = (
        P(("row", "col"), None),
        P(),
        P("row", "col", None, None, None, None),
        P("row", "col", None, None),
        P("row", "col", None, None),
        P("row", "col", None),
        P(("row", "col")),
        P(("row", "col"), None),
    )
    out_specs = (P(("row", "col"), None), P(("row", "col"), None), P())
    return jax.shard_map(body, mesh=mesh, in_specs=in_specs, out_specs=out_specs, check_vma=False)
```

```python
import functools
import math

import jax
import jax.numpy as jnp
from jax import lax
from jax.experimental import pallas as pl
from jax.experimental.pallas import tpu as pltpu
from jax.sharding import PartitionSpec as P

BF16 = jnp.bfloat16
F32 = jnp.float32


def layer_kernel(
    row_count,
    col_count,
    grad_scale,
    halves,
    trow_ref,
    tcol_ref,
    tcount_ref,
    adj_ref,
    feat_ref,
    weight_ref,
    mask_ref,
    cot_ref,
    hidden_ref,
    gfeat_ref,
    gweight_ref,
    tiles,
    dense,
    held,
    acc,
    col_out,
    col_in,
    grad_t,
    grad_cat,
    core_out,
    core_in,
    mate_out,
    mate_in,
    line_out,
    line_in,
    own_sum,
    proj_t,
    feat_pad,
    gw_loc,
    gw_s2,
    gw_r2,
    gw_line,
    gw_full,
    adj_sem,
    g_line,
    g_mate,
    g_core,
    g_recv,
    c_send,
    c_recv,
    t_send,
    t_recv,
    b_core_send,
    b_core_recv,
    b_mate_send,
    b_mate_recv,
    b_line_send,
    b_line_recv,
    w_plane_send,
    w_plane_recv,
    w_line_send,
    w_line_recv,
    w_gat_send,
    w_gat_recv,
):
    line_count = row_count // 4
    me = lax.axis_index("row")
    col = lax.axis_index("col")
    core = me % 2
    mate = (me // 2) % 2
    line = me // 4
    slot_count = adj_ref.shape[3]
    tile = adj_ref.shape[4]
    nodes = feat_ref.shape[1]
    block_tiles = nodes // tile
    hid = weight_ref.shape[1] // halves

    def row_id(l, m, k):
        return (l * 2 + m) * 2 + k

    def line_at(d):
        return (line + d) % line_count

    to_core = {"row": row_id(line, mate, 1 - core)}
    to_mate = {"row": row_id(line, 1 - mate, core)}

    def to_line(d):
        return {"row": row_id(line_at(d), mate, core)}

    def to_col(d):
        return {"col": (col + d) % col_count}

    plane = [
        (dk, dm, dc) for dk in range(2) for dm in range(2) for dc in range(col_count)
    ][1:]

    def plane_offset(dk, dm, dc):
        return (dk * 2 + dm) * col_count + dc

    def plane_part(dk, dm, dc):
        return plane_offset((core + dk) % 2, (mate + dm) % 2, (col + dc) % col_count)

    def to_plane(dk, dm, dc):
        return {
            "row": row_id(line, (mate + dm) % 2, (core + dk) % 2),
            "col": (col + dc) % col_count,
        }

    near = sorted(range(1, line_count), key=lambda d: min(d, line_count - d))
    far = near[::-1]
    peers = [to_plane(*step) for step in plane] + [to_line(d) for d in near]

    started = []

    def push(src, dst, send, recv, target):
        copy = pltpu.make_async_remote_copy(
            src_ref=src,
            dst_ref=dst,
            send_sem=send,
            recv_sem=recv,
            device_id=target,
            device_id_type=pl.DeviceIdType.MESH,
        )
        copy.start()
        started.append(copy)

    def arrived(dst, recv):
        pltpu.make_async_remote_copy(
            src_ref=dst,
            dst_ref=dst,
            send_sem=recv,
            recv_sem=recv,
            device_id=to_core,
            device_id_type=pl.DeviceIdType.MESH,
        ).wait_recv()

    adj_copy = pltpu.make_async_copy(
        adj_ref.at[0, 0], tiles.at[:, pl.ds(0, slot_count)], adj_sem
    )
    adj_copy.start()
    barrier = pltpu.get_barrier_semaphore()
    for peer in peers:
        pl.semaphore_signal(
            barrier, inc=1, device_id=peer, device_id_type=pl.DeviceIdType.MESH
        )
    projected = lax.dot_general(
        feat_ref[...], weight_ref[...], (((0,), (0,)), ((), ())), preferred_element_type=F32
    ).astype(BF16)
    for h in range(halves):
        held[h, me] = projected[:, h * hid : (h + 1) * hid]
    pl.semaphore_wait(barrier, len(peers))

    def send_own(h):
        own = held.at[h, me]
        for d in near:
            push(own, own, g_line.at[h, d], g_recv.at[h, me], to_line(d))
        push(own, own, g_mate.at[h, line], g_recv.at[h, me], to_mate)
        push(own, own, g_core.at[h, line * 2 + mate], g_recv.at[h, me], to_core)

    send_own(0)
    tiles[:, slot_count] = jnp.zeros_like(tiles[:, slot_count])
    adj_copy.wait()

    def build(j, carry):
        filled = []
        for s in range(slot_count):
            live = s < tcount_ref[0, 0, j]
            place = trow_ref[0, s, 0, j] * block_tiles + tcol_ref[0, s, 0, j]
            filled.append(jnp.where(live, place, -1))
        for r in range(col_count * block_tiles):
            for t in range(block_tiles):
                slot = jnp.int32(slot_count)
                for s in range(slot_count):
                    slot = jnp.where(filled[s] == r * block_tiles + t, s, slot)
                dense[j, pl.ds(r * tile, tile), pl.ds(t * tile, tile)] = tiles[j, slot]
        return carry

    if halves == 1:
        lax.fori_loop(0, row_count, build, 0)

    def rows_of(i):
        return pl.ds(pl.multiple_of(i * nodes, nodes), nodes)

    def accumulate(h, j, first=False):
        if halves > 1 and h == 0:
            build(j, 0)
        if col_count <= 2:
            product = jnp.dot(dense[j], held[h, j], preferred_element_type=F32)
            acc[h] = product if first else acc[h] + product
            return

        def one(i, carry):
            product = jnp.dot(dense[j, rows_of(i)], held[h, j], preferred_element_type=F32)
            acc[h, rows_of(i)] = product if first else acc[h, rows_of(i)] + product
            return carry

        lax.fori_loop(0, col_count, one, 0)

    def forward_mate(h, l):
        block = row_id(l, mate, core)
        ref = held.at[h, block]
        push(ref, ref, g_mate.at[h, l], g_recv.at[h, block], to_mate)

    def forward_core(h, l, m):
        block = row_id(l, m, core)
        ref = held.at[h, block]
        push(ref, ref, g_core.at[h, l * 2 + m], g_recv.at[h, block], to_core)

    def take(h, l, m, k):
        block = row_id(l, m, k)
        arrived(held.at[h, block], g_recv.at[h, block])
        return block

    def gather_steps(h):
        accumulate(h, me, first=True)
        if h + 1 < halves:
            send_own(h + 1)
        accumulate(h, take(h, line, mate, 1 - core))
        late = []
        last_line = line
        for d in near:
            l = line_at(d)
            block = take(h, l, mate, core)
            forward_mate(h, l)
            forward_core(h, l, mate)
            crossed = take(h, last_line, 1 - mate, core)
            forward_core(h, last_line, 1 - mate)
            for item in late:
                accumulate(h, take(h, *item))
            accumulate(h, block)
            accumulate(h, crossed)
            late = [(l, mate, 1 - core), (last_line, 1 - mate, 1 - core)]
            last_line = l
            yield
        for item in late:
            accumulate(h, take(h, *item))
        crossed = take(h, last_line, 1 - mate, core)
        forward_core(h, last_line, 1 - mate)
        accumulate(h, crossed)
        accumulate(h, take(h, last_line, 1 - mate, 1 - core))

    def col_send(h):
        for d in range(1, col_count):
            col_out[h, d] = acc[h, rows_of((col + d) % col_count)].astype(BF16)
            push(col_out.at[h, d], col_in.at[h, d], c_send.at[h, d], c_recv.at[h, d], to_col(d))

    def col_finish(h):
        lanes = slice(h * hid, (h + 1) * hid)
        pre_act = acc[h, rows_of(col)]
        for d in range(1, col_count):
            arrived(col_in.at[h, d], c_recv.at[h, d])
            pre_act = pre_act + col_in[h, d].astype(F32)
        gate = jax.nn.sigmoid(pre_act)
        grad_pre = cot_ref[:, lanes].astype(F32) * gate * (1.0 + pre_act * (1.0 - gate))
        grad_t[h, col] = (grad_pre.T * mask_ref[...].astype(F32)).astype(BF16)
        mine = grad_t.at[h, col]
        for d in range(1, col_count):
            push(mine, mine, t_send.at[h, d], t_recv.at[h, col], to_col(d))
        hidden_ref[:, lanes] = (pre_act * gate).astype(BF16)

    def col_take(h):
        for d in range(1, col_count):
            other = (col + d) % col_count
            arrived(grad_t.at[h, other], t_recv.at[h, other])
        for i in range(col_count):
            grad_cat[h, :, i * nodes : (i + 1) * nodes] = grad_t[h, i]

    def partial_sum(h, block):
        if col_count <= 2:
            return jnp.dot(grad_cat[h], dense[block], preferred_element_type=F32)

        def one(i, running):
            return running + jnp.dot(
                grad_t[h, i], dense[block, rows_of(i)], preferred_element_type=F32
            )

        return lax.fori_loop(0, col_count, one, jnp.zeros((hid, nodes), F32))

    order = far + [0]

    def send_core(h, side):
        for d in order:
            l = line_at(d)
            at = l * 2 + side
            core_out[h, at] = partial_sum(h, row_id(l, side, 1 - core)).astype(BF16)
            push(
                core_out.at[h, at],
                core_in.at[h, at],
                b_core_send.at[h, at],
                b_core_recv.at[h, at],
                to_core,
            )

    def send_mate(h):
        for d in order:
            l = line_at(d)
            at = l * 2 + 1 - mate
            mine = partial_sum(h, row_id(l, 1 - mate, core))
            arrived(core_in.at[h, at], b_core_recv.at[h, at])
            mate_out[h, l] = (mine + core_in[h, at].astype(F32)).astype(BF16)
            push(
                mate_out.at[h, l],
                mate_in.at[h, l],
                b_mate_send.at[h, l],
                b_mate_recv.at[h, l],
                to_mate,
            )

    def send_line(h):
        for d in order:
            l = line_at(d)
            at = l * 2 + mate
            mine = partial_sum(h, row_id(l, mate, core))
            arrived(core_in.at[h, at], b_core_recv.at[h, at])
            mine = mine + core_in[h, at].astype(F32)
            arrived(mate_in.at[h, l], b_mate_recv.at[h, l])
            mine = mine + mate_in[h, l].astype(F32)
            if d:
                line_out[h, d] = mine.astype(BF16)
                push(
                    line_out.at[h, d],
                    line_in.at[h, d],
                    b_line_send.at[h, d],
                    b_line_recv.at[h, d],
                    to_line(d),
                )
            else:
                own_sum[h] = mine

    def finish(h):
        total = own_sum[h]
        for d in far:
            arrived(line_in.at[h, d], b_line_recv.at[h, d])
            total = total + line_in[h, d].astype(F32)
        proj_t[h * hid : (h + 1) * hid, :] = total.astype(BF16)

    def pad_features():
        width = feat_ref.shape[0]
        pad_from = (width // 16) * 16
        feat_pad[pad_from:, :] = jnp.zeros_like(feat_pad[pad_from:, :])
        feat_pad[:width, :] = feat_ref[...]

    wire = gw_full.dtype

    def weight_steps(h):
        local = lax.dot_general(
            proj_t[h * hid : (h + 1) * hid, :],
            feat_pad[...],
            (((1,), (1,)), ((), ())),
            preferred_element_type=F32,
        )
        gw_loc[h] = (local * grad_scale).reshape(gw_loc.shape[1:])
        for step in plane[::-1]:
            at = plane_offset(*step)
            gw_s2[h, at] = gw_loc[h, plane_part(*step)].astype(wire)
            push(
                gw_s2.at[h, at],
                gw_r2.at[h, at],
                w_plane_send.at[h, at],
                w_plane_recv.at[h, at],
                to_plane(*step),
            )
        own_part = plane_part(0, 0, 0)
        part = gw_loc[h, own_part]
        yield
        for step in plane:
            at = plane_offset(*step)
            arrived(gw_r2.at[h, at], w_plane_recv.at[h, at])
            part = part + gw_r2[h, at].astype(F32)
        gw_line[h, line] = part.astype(wire)
        mine = gw_line.at[h, line]
        for d in far:
            push(mine, mine, w_line_send.at[h, d], w_line_recv.at[h, line], to_line(d))
        yield
        for d in near:
            l = line_at(d)
            arrived(gw_line.at[h, l], w_line_recv.at[h, l])
        part = gw_line[h, 0].astype(F32)
        for i in range(1, line_count):
            part = part + gw_line[h, i].astype(F32)
        gw_full[h, own_part] = part.astype(wire)
        mine = gw_full.at[h, own_part]
        for step in plane[::-1]:
            push(
                mine,
                mine,
                w_gat_send.at[h, plane_offset(*step)],
                w_gat_recv.at[h, own_part],
                to_plane(*step),
            )
        yield
        for step in plane:
            p = plane_part(*step)
            arrived(gw_full.at[h, p], w_gat_recv.at[h, p])
        full = gw_full[h].reshape(hid, gweight_ref.shape[0])
        gweight_ref[:, h * hid : (h + 1) * hid] = full.T

    def feature_gradient():
        gfeat_ref[...] = jnp.dot(
            weight_ref[...], proj_t[...], preferred_element_type=F32
        ).astype(BF16)

    if halves == 2:
        first, second = gather_steps(0), gather_steps(1)
        for _ in near:
            next(first)
        next(second)
        for _ in first:
            pass
        col_send(0)
        next(second)
        pad_features()
        col_finish(0)
        for _ in second:
            pass
        col_send(1)
        col_take(0)
        send_core(0, 1 - mate)
        col_finish(1)
        send_mate(0)
        send_core(0, mate)
        col_take(1)
        send_core(1, 1 - mate)
        send_line(0)
        send_mate(1)
        send_core(1, mate)
        send_line(1)
        finish(0)
        ahead, behind = weight_steps(0), weight_steps(1)
        next(ahead)
        finish(1)
        next(behind)
        for _ in ahead:
            next(behind)
        feature_gradient()
        for _ in behind:
            pass
    else:
        for _ in gather_steps(0):
            pass
        col_send(0)
        pad_features()
        col_finish(0)
        col_take(0)
        send_core(0, 1 - mate)
        send_mate(0)
        send_core(0, mate)
        send_line(0)
        finish(0)
        steps = weight_steps(0)
        next(steps)
        feature_gradient()
        for _ in steps:
            pass

    for copy in started:
        copy.wait_send()


def results_kernel(hidden_in, gfeat_in, gweight_in, hidden_ref, gfeat_ref, gweight_ref):
    hidden_ref[...] = hidden_in[...]
    gfeat_ref[...] = gfeat_in[...]
    gweight_ref[...] = gweight_in[: gweight_ref.shape[0], :].astype(F32)


def body(features, weight, adj_tiles, tile_row, tile_col, tile_count, train_mask, cotangent):
    rows = lax.axis_size("row")
    cols = lax.axis_size("col")
    slot_count, tile = adj_tiles.shape[3], adj_tiles.shape[4]
    nodes, width = features.shape
    hid = weight.shape[1]
    lines = rows // 4
    padded = -(-width // 128) * 128
    parts = 4 * cols
    halves = 2 if hid % (16 * parts) == 0 and cols <= 2 else 1
    part_hid = hid // halves
    piece = part_hid // parts
    wire = BF16 if piece % 16 == 0 else F32
    grad_scale = 1.0 / math.sqrt(rows * cols * nodes)

    vmem = pltpu.VMEM
    half_sems = lambda n: pltpu.SemaphoreType.DMA((halves, n))
    scratch = [
        vmem((rows, slot_count + 1, tile, tile), BF16),
        vmem((rows, cols * nodes, nodes), BF16),
        vmem((halves, rows, nodes, part_hid), BF16),
        vmem((halves, cols * nodes, part_hid), F32),
        vmem((halves, cols, nodes, part_hid), BF16),
        vmem((halves, cols, nodes, part_hid), BF16),
        vmem((halves, cols, part_hid, nodes), BF16),
        vmem((halves, part_hid, cols * nodes), BF16),
        vmem((halves, rows // 2, part_hid, nodes), BF16),
        vmem((halves, rows // 2, part_hid, nodes), BF16),
        vmem((halves, lines, part_hid, nodes), BF16),
        vmem((halves, lines, part_hid, nodes), BF16),
        vmem((halves, lines, part_hid, nodes), BF16),
        vmem((halves, lines, part_hid, nodes), BF16),
        vmem((halves, part_hid, nodes), F32),
        vmem((hid, nodes), BF16),
        vmem((padded, nodes), BF16),
        vmem((halves, parts, piece, padded), F32),
        vmem((halves, parts, piece, padded), wire),
        vmem((halves, parts, piece, padded), wire),
        vmem((halves, lines, piece, padded), wire),
        vmem((halves, parts, piece, padded), wire),
        pltpu.SemaphoreType.DMA,
        half_sems(lines),
        half_sems(lines),
        half_sems(rows // 2),
        half_sems(rows),
        half_sems(cols),
        half_sems(cols),
        half_sems(cols),
        half_sems(cols),
        half_sems(rows // 2),
        half_sems(rows // 2),
        half_sems(lines),
        half_sems(lines),
        half_sems(lines),
        half_sems(lines),
        half_sems(parts),
        half_sems(parts),
        half_sems(lines),
        half_sems(lines),
        half_sems(parts),
        half_sems(parts),
    ]
    whole = pl.BlockSpec(memory_space=pltpu.VMEM)
    hidden, grad_features, grad_weight = pl.pallas_call(
        functools.partial(layer_kernel, rows, cols, grad_scale, halves),
        out_shape=(
            jax.ShapeDtypeStruct((nodes, hid), BF16),
            jax.ShapeDtypeStruct((width, nodes), BF16),
            jax.ShapeDtypeStruct((padded, hid), wire),
        ),
        in_specs=[
            pl.BlockSpec(memory_space=pltpu.SMEM),
            pl.BlockSpec(memory_space=pltpu.SMEM),
            pl.BlockSpec(memory_space=pltpu.SMEM),
            pl.BlockSpec(memory_space=pl.ANY),
            whole,
            whole,
            whole,
            whole,
        ],
        out_specs=(whole, whole, whole),
        scratch_shapes=scratch,
        compiler_params=pltpu.CompilerParams(
            collective_id=0, has_side_effects=True, vmem_limit_bytes=63 * 1024 * 1024
        ),
        name="graph_layer",
    )(
        tile_row.transpose(0, 3, 1, 2),
        tile_col.transpose(0, 3, 1, 2),
        tile_count,
        adj_tiles,
        features.T,
        weight,
        train_mask.reshape(1, nodes),
        cotangent,
    )
    hidden, grad_features, grad_weight = pl.pallas_call(
        results_kernel,
        out_shape=(
            jax.ShapeDtypeStruct((nodes, hid), BF16),
            jax.ShapeDtypeStruct((width, nodes), BF16),
            jax.ShapeDtypeStruct((width, hid), F32),
        ),
        in_specs=[whole] * 3,
        out_specs=(whole, whole, whole),
        name="results",
    )(hidden, grad_features, grad_weight)
    return (hidden, grad_features.T, grad_weight)


def solution(mesh):
    in_specs = (
        P(("row", "col"), None),
        P(),
        P("row", "col", None, None, None, None),
        P("row", "col", None, None),
        P("row", "col", None, None),
        P("row", "col", None),
        P(("row", "col")),
        P(("row", "col"), None),
    )
    out_specs = (P(("row", "col"), None), P(("row", "col"), None), P())
    return jax.shard_map(body, mesh=mesh, in_specs=in_specs, out_specs=out_specs, check_vma=False)
```
